512 devices in a mesh: bulk: 32 (over z, y_lo), group: 16 (over y_hi, x, core).
Axes of the slice: x: 4, y: 4 (y_hi: 2, y_lo: 2; y = y_hi * 2 + y_lo), z: 16, core: 2. Of those that a mesh axis runs over, the one named last changes fastest.
Arguments:
- snapshots: bfloat16 [3145728, 128], P(('bulk', 'group'))
- owned_rows: int32 [512], P(('bulk', 'group')), may hold values from 3072 to 6144, as said below
- iface_lists: int32 [512, 4, 512], P(('bulk', 'group')), may hold values from 0 to 6143, as said below
- block_columns: int32 [49152, 9], P(('bulk', 'group')), may hold values from 0 to 127, as said below
- block_types: int32 [49152, 9], P(('bulk', 'group')), may hold values from 0 to 15
- block_scales: float32 [49152, 9], P(('bulk', 'group')), may hold values from 0.2 to 0.8
- mass_table: bfloat16 [16, 64, 64], replicated
- sketch_matrix: bfloat16 [128, 256], replicated, may hold values from -0.5 to 0.5
Outputs:
- projected: bfloat16 [3145728, 256], P(('bulk', 'group'))
- sketch: float32 [128, 256], replicated
The draws below stay inside these ranges and needn't reach their ends.
Inputs may be any that keep to these rules, and one draw needn't show every extreme that they name: Partition p owns its first owned_rows[p] rows; the rest of its 6144 rows are padding. Some partition owns all 6144. iface_lists[p, d] lists, with possible repeats, local owned rows of partition p (each below owned_rows[p]) for its neighbour d: 0 and 1 the lower and upper one along bulk, 2 and 3 the lower and upper one along group. `block_columns`: block row i of partition p names own block j < 96 or ghost block 96 + j; every ghost block is named by some block row of every partition.
All inputs are finite; a program needn't handle non-finite values.
Results may differ from the reference program's by a relative error of at most 0.0041.
The reference program's roundings to bfloat16 on the way (of `panel`, `ghosts` and `weighted`) count: a program that leaves them out, or rounds other values in their place, can miss the bound.
Values may be sent and summed in bfloat16 or wider, within the bound.
A program may use at most 64 MiB of HBM per device.

```python
import math
import jax
import jax.numpy as jnp
from jax import lax

SNAP = 128
SKETCH = 256
BLOCK = 64
K = 9
NT = 16
ROWS = 6144
IF = 512
NB = 96
GB = 32
PARTS_SIZE = 512
NODES = 3145728
BROWS = 49152
N_BULK = 32
N_GROUP = 16


def part_counts(key):
    key = jax.random.fold_in(key, 101)
    first_key, second_key = jax.random.split(key)
    counts = jax.random.randint(first_key, (PARTS_SIZE,), ROWS // 2, ROWS + 1)
    full_part = jax.random.randint(second_key, (), 0, PARTS_SIZE)
    slots = jnp.arange(PARTS_SIZE)
    counts = jnp.where(slots == full_part, ROWS, counts)
    counts = jnp.where(slots == (full_part + 1) % PARTS_SIZE, ROWS // 2, counts)
    return (counts.astype(jnp.int32), full_part)


def draw_owned_rows(key, part):
    counts, full_part = part_counts(key)
    return counts


def draw_iface_lists(key, part):
    counts, full_part = part_counts(key)
    key = jax.random.fold_in(key, 7)
    lists = jax.random.randint(key, (PARTS_SIZE, 4, IF), 0, counts[:, None, None])
    corner = (jnp.arange(PARTS_SIZE)[:, None, None] == full_part) & (jnp.arange(4)[None, :, None] == 0) & (jnp.arange(IF)[None, None, :] == 0)
    return jnp.where(corner, ROWS - 1, lists).astype(jnp.int32)


def draw_block_columns(key, part):
    key = jax.random.fold_in(key, 11)
    base_key, perm_key, place_key = jax.random.split(key, 3)
    base = jax.random.randint(base_key, (PARTS_SIZE, NB, K), 0, NB + GB)
    orders = jax.vmap(lambda one_key: jax.random.permutation(one_key, NB))(jax.random.split(perm_key, PARTS_SIZE))
    place = jax.random.randint(place_key, (PARTS_SIZE, NB, 1), 0, K)
    chosen = (jnp.arange(K)[None, None, :] == place) & (orders[:, :, None] < GB)
    columns = jnp.where(chosen, NB + orders[:, :, None], base)
    return columns.reshape(PARTS_SIZE * NB, K).astype(jnp.int32)


def draw_mass_table(key, part):
    key = jax.random.fold_in(key, 13)
    diag_key, off_key = jax.random.split(key)
    diagonal = jax.random.uniform(diag_key, (NT, BLOCK, BLOCK), jnp.float32, 0.8, 1.5)
    spread = jax.random.normal(off_key, (NT, BLOCK, BLOCK), jnp.float32) * (0.35 / math.sqrt(BLOCK))
    on_diag = jnp.arange(BLOCK)[:, None] == jnp.arange(BLOCK)[None, :]
    return jnp.where(on_diag[None], diagonal, spread).astype(jnp.bfloat16)


def draw_snapshots(key, part):
    key = jax.random.fold_in(key, 3)
    value_key, scale_key = jax.random.split(key, 2)
    position = jnp.arange(NODES, dtype=jnp.float32)[:, None] / (NODES - 1)
    ramp = 1.0 + 2.0 * position
    rough = jnp.exp(jax.random.uniform(scale_key, (NODES, 1), jnp.float32, math.log(0.3), math.log(3.0)))
    values = jax.random.normal(value_key, (NODES, SNAP), jnp.float32)
    return (values * ramp * rough).astype(jnp.bfloat16)


def with_ends(drawn, stream_key, low, high):
    longest = drawn.shape.index(max(drawn.shape))
    spots = []
    for shift in (0, 1):
        where = [jax.random.randint(jax.random.fold_in(stream_key, axis), (), 0, length) for axis, length in enumerate(drawn.shape)]
        where[longest] = (where[longest] + shift) % drawn.shape[longest]
        spots.append(tuple(where))
    return drawn.at[spots[0]].set(low).at[spots[1]].set(high)


def level_of(stream_key, shape, shards, smallest, largest):
    def one(dim, blocks):
        heights = jax.random.uniform(jax.random.fold_in(jax.random.fold_in(stream_key, 6), dim), (blocks,), jnp.float32, smallest / len(shards), largest / len(shards))
        return jnp.repeat(jnp.exp(heights), shape[dim] // blocks).reshape((-1,) + (1,) * (len(shape) - dim - 1))

    loudness = one(*shards[0])
    for cut in shards[1:]:
        loudness = loudness * one(*cut)
    return loudness


def centred(own_key, shape, scale, limit, held_as=jnp.bfloat16):
    return jnp.clip(scale * jax.random.normal(own_key, shape, jnp.float32), -limit, limit).astype(held_as)


def setup_inputs(seed: int = 0) -> dict:
    streams_of = jax.random.split(jax.random.key(seed), 9)
    snapshots = draw_snapshots(jax.random.fold_in(streams_of[8], 71), 0)
    owned_rows = draw_owned_rows(jax.random.fold_in(streams_of[8], 71), 0)
    iface_lists = draw_iface_lists(jax.random.fold_in(streams_of[8], 71), 0)
    block_columns = draw_block_columns(jax.random.fold_in(streams_of[8], 71), 0)
    block_types = with_ends(jax.random.randint(streams_of[4], (BROWS, K), 0, NT), jax.random.fold_in(streams_of[4], 1), 0, NT - 1).astype(jnp.int32)
    block_scales = jnp.clip(jnp.exp(math.log(0.8) - 1.3862944 * jax.random.uniform(streams_of[5], (BROWS, K), jnp.float32) ** level_of(streams_of[5], (BROWS, K), ((0, 512),), -0.2, 0.2)), 0.2, 0.8)
    mass_table = draw_mass_table(jax.random.fold_in(streams_of[8], 71), 0)
    sketch_matrix = centred(streams_of[7], (SNAP, SKETCH), SNAP ** -0.5, 0.5)
    return {"snapshots": snapshots, "owned_rows": owned_rows, "iface_lists": iface_lists, "block_columns": block_columns, "block_types": block_types, "block_scales": block_scales, "mass_table": mass_table, "sketch_matrix": sketch_matrix}


def pick_rows(panel_rows, list_rows):
    return panel_rows[list_rows]


def reference(snapshots, owned_rows, iface_lists, block_columns, block_types, block_scales, mass_table, sketch_matrix):
    panel = snapshots.reshape(N_BULK, N_GROUP, ROWS, SNAP)
    owned_mask = jnp.arange(ROWS)[None, None, :] < owned_rows.reshape(N_BULK, N_GROUP)[:, :, None]
    panel = jnp.where(owned_mask[..., None], panel, jnp.zeros((), jnp.bfloat16))
    lists = iface_lists.reshape(N_BULK, N_GROUP, 4, IF)
    outgoing = jax.vmap(jax.vmap(pick_rows))(panel, lists)
    zero_plane = jnp.zeros((1, N_GROUP, IF, SNAP), jnp.bfloat16)
    from_lower = jnp.concatenate([zero_plane, outgoing[:-1, :, 1]], axis=0)
    from_upper = jnp.concatenate([outgoing[1:, :, 0], zero_plane], axis=0)
    from_left = jnp.roll(outgoing[:, :, 3], 1, axis=1)
    from_right = jnp.roll(outgoing[:, :, 2], -1, axis=1)
    ghosts = jnp.concatenate([from_lower, from_upper, from_left, from_right], axis=2)
    stacked = jnp.concatenate([panel, ghosts], axis=2).reshape(PARTS_SIZE, ROWS + 4 * IF, SNAP)
    mask_rows = owned_mask.reshape(PARTS_SIZE, ROWS)
    column_ids = block_columns.reshape(PARTS_SIZE, NB, K)
    type_ids = block_types.reshape(PARTS_SIZE, NB, K)
    jacobians = block_scales.reshape(PARTS_SIZE, NB, K)

    def part_terms(inputs):
        node_rows, row_mask, part_columns, part_types, part_scales = inputs
        node_blocks = node_rows.reshape(NB + GB, BLOCK, SNAP)

        def add_entry(entry_index, accumulated):
            blocks_f = node_blocks[part_columns[:, entry_index]].astype(jnp.float32)
            tiles_f = mass_table[part_types[:, entry_index]].astype(jnp.float32)
            term_value = jnp.einsum('bij,bjs->bis', tiles_f, blocks_f)
            return accumulated + part_scales[:, entry_index][:, None, None] * term_value

        accumulated = lax.fori_loop(0, K, add_entry, jnp.zeros((NB, BLOCK, SNAP), jnp.float32))
        weighted = jnp.where(row_mask[:, None], accumulated.reshape(ROWS, SNAP), jnp.zeros((), jnp.float32)).astype(jnp.bfloat16)
        projected = jnp.dot(weighted, sketch_matrix, preferred_element_type=jnp.float32).astype(jnp.bfloat16)
        own_rows = node_rows[:ROWS]
        local_gram = jnp.dot(own_rows.T, weighted, preferred_element_type=jnp.float32)
        return projected, local_gram

    projected, grams = lax.map(part_terms, (stacked, mask_rows, column_ids, type_ids, jacobians))
    gram_total = jnp.sum(grams, axis=0)
    sketch = jnp.dot(gram_total, sketch_matrix.astype(jnp.float32), precision=lax.Precision.HIGHEST) / ROWS
    return projected.reshape(NODES, SKETCH), sketch
```

```python
import functools

import jax
import jax.numpy as jnp
from jax import lax
from jax.experimental import pallas as pl
from jax.experimental.pallas import tpu as pltpu
from jax.sharding import PartitionSpec as P

MESH = pl.DeviceIdType.MESH
NEAR = 2
MIB = 1 << 20


def rows_kernel(
    bulk_n, group_n, lists, snap_hbm, ghosts, snap, wide, picked, packed, load_sem, send_sem, recv_sem
):
    row_count = snap.shape[0]
    faces = packed.shape[1]
    b, g = lax.axis_index("bulk"), lax.axis_index("group")
    above, below = lax.rem(b + 1, bulk_n), lax.rem(b + bulk_n - 1, bulk_n)
    right, left = lax.rem(g + 1, group_n), lax.rem(g + group_n - 1, group_n)
    plan = ((1, (above, g)), (0, (below, g)), (3, (b, right)), (2, (b, left)))

    load = pltpu.make_async_copy(snap_hbm, snap, load_sem)
    load.start()
    barrier = pltpu.get_barrier_semaphore()
    for _, peer in plan:
        pl.semaphore_signal(barrier, inc=1, device_id=peer, device_id_type=MESH)
    load.wait()
    step = 256

    def widen(i, carry):
        rows = pl.ds(pl.multiple_of(i * step, step), step)
        wide[rows, :] = snap[rows, :].astype(jnp.float32)
        return carry

    lax.fori_loop(0, row_count // step, widen, 0)
    pl.semaphore_wait(barrier, len(plan))

    copies = []
    for slot, (which, peer) in enumerate(plan):

        def pick(i, carry):
            for u in range(16):
                r = i * 16 + u
                picked[pl.ds(r, 1), :] = wide[pl.ds(lists[0, which, r], 1), :]
            return carry

        lax.fori_loop(0, faces // 16, pick, 0)
        packed[slot] = picked[...].astype(jnp.bfloat16)
        copy = pltpu.make_async_remote_copy(
            src_ref=packed.at[slot],
            dst_ref=ghosts.at[slot],
            send_sem=send_sem.at[slot],
            recv_sem=recv_sem.at[slot],
            device_id=peer,
            device_id_type=MESH,
        )
        copy.start()
        copies.append(copy)
    for copy in copies:
        copy.wait()


def exchanged(snapshots, iface_lists, bulk_n, group_n):
    rows, snaps = snapshots.shape
    faces = iface_lists.shape[2]
    return pl.pallas_call(
        functools.partial(rows_kernel, bulk_n, group_n),
        out_shape=jax.ShapeDtypeStruct((4, faces, snaps), jnp.bfloat16),
        in_specs=[pl.BlockSpec(memory_space=pltpu.SMEM), pl.BlockSpec(memory_space=pl.ANY)],
        out_specs=pl.BlockSpec(memory_space=pl.ANY),
        scratch_shapes=[
            pltpu.VMEM((rows, snaps), jnp.bfloat16),
            pltpu.VMEM((rows, snaps), jnp.float32),
            pltpu.VMEM((faces, snaps), jnp.float32),
            pltpu.VMEM((4, faces, snaps), jnp.bfloat16),
            pltpu.SemaphoreType.DMA,
            pltpu.SemaphoreType.DMA((4,)),
            pltpu.SemaphoreType.DMA((4,)),
        ],
        compiler_params=pltpu.CompilerParams(
            collective_id=0, has_side_effects=True, vmem_limit_bytes=24 * MIB
        ),
        name="ghost_rows",
    )(iface_lists, snapshots)


def mass_kernel(
    edges, entries, owned, columns, types, scales, snap, ghosts, table, test,
    projected, gram, cols, pairs, weighted, total,
):
    step, steps = pl.program_id(0), pl.num_programs(0)
    own, block, snaps = snap.shape
    outer = ghosts.shape[0]
    per_step = projected.shape[0] // block
    lane = lax.broadcasted_iota(jnp.int32, (1, 2 * block), 1) < block
    line = lax.broadcasted_iota(jnp.int32, (block, snaps), 0)
    count = owned[0]

    @pl.when(step == 0)
    def _():
        b = lax.axis_index("bulk")
        total[...] = jnp.zeros_like(total)
        for t in range(table.shape[0]):
            both = table[t].astype(jnp.float32)
            pairs[t] = jnp.concatenate([both, both], axis=1)

        def own_blocks(i, carry):
            keep = line + i * block < count
            cols[i] = jnp.where(keep, snap[i].astype(jnp.float32), 0.0).astype(jnp.bfloat16)
            return carry

        def ghost_blocks(i, carry):
            side = i // (outer // 4)
            gone = ((side == 0) & (b == 0)) | ((side == 1) & (b == edges - 1))
            value = ghosts[i].astype(jnp.float32)
            keep = line < jnp.where(gone, 0, block)
            cols[own + i] = jnp.where(keep, value, 0.0).astype(jnp.bfloat16)
            return carry

        lax.fori_loop(0, own, own_blocks, 0)
        lax.fori_loop(0, outer, ghost_blocks, 0)

    for u in range(per_step):
        r = step * per_step + u
        tiles = []
        for k in range(0, entries - 1, 2):
            one, two = pairs[types[k, r]], pairs[types[k + 1, r]]
            factor = jnp.where(lane, scales[k, r], scales[k + 1, r])
            tiles.append((jnp.where(lane, one, two) * factor).astype(jnp.bfloat16))
        if entries % 2:
            last = pairs[types[entries - 1, r]][:, :block] * scales[entries - 1, r]
            tiles.append(last.astype(jnp.bfloat16))
        stacked = jnp.concatenate([cols[columns[k, r]] for k in range(entries)], axis=0)
        value = jnp.dot(
            jnp.concatenate(tiles, axis=1), stacked, preferred_element_type=jnp.float32
        )
        keep = line + r * block < count
        weighted[u * block : (u + 1) * block, :] = jnp.where(keep, value, 0.0).astype(jnp.bfloat16)

    here = weighted[...]
    projected[...] = jnp.dot(here, test[...], preferred_element_type=jnp.float32).astype(jnp.bfloat16)
    mine = snap[pl.ds(step * per_step, per_step)].reshape(per_step * block, snaps)
    total[...] += lax.dot_general(
        mine, here, (((0,), (0,)), ((), ())), preferred_element_type=jnp.float32
    )

    @pl.when(step == steps - 1)
    def _():
        parts, height = gram.shape[0], gram.shape[1]
        for p in range(parts):
            gram[p] = total[p * height : (p + 1) * height, :]


def mass_product(owned, columns, types, scales, snapshots, ghosts, table, test, edges, parts):
    rows, snaps = snapshots.shape
    kinds, block, _ = table.shape
    own, outer = rows // block, ghosts.shape[0] * ghosts.shape[1] // block
    entries = columns.shape[1]
    width = test.shape[1]
    per_step = 8
    whole = lambda shape: pl.BlockSpec(shape, lambda i: (0,) * len(shape))
    scalar = pl.BlockSpec(memory_space=pltpu.SMEM)
    return pl.pallas_call(
        functools.partial(mass_kernel, edges, entries),
        grid=(own // per_step,),
        out_shape=(
            jax.ShapeDtypeStruct((rows, width), jnp.bfloat16),
            jax.ShapeDtypeStruct((parts, snaps // parts, snaps), jnp.float32),
        ),
        in_specs=[
            scalar, scalar, scalar, scalar,
            whole((own, block, snaps)),
            whole((outer, block, snaps)),
            whole((kinds, block, block)),
            whole((snaps, width)),
        ],
        out_specs=(
            pl.BlockSpec((per_step * block, width), lambda i: (i, 0)),
            whole((parts, snaps // parts, snaps)),
        ),
        scratch_shapes=[
            pltpu.VMEM((own + outer, block, snaps), jnp.bfloat16),
            pltpu.VMEM((kinds, block, 2 * block), jnp.float32),
            pltpu.VMEM((per_step * block, snaps), jnp.bfloat16),
            pltpu.VMEM((snaps, snaps), jnp.float32),
        ],
        compiler_params=pltpu.CompilerParams(vmem_limit_bytes=32 * MIB),
        name="mass_product",
    )(
        owned, columns.T, types.T, scales.T,
        snapshots.reshape(own, block, snaps),
        ghosts.reshape(outer, block, snaps),
        table, test,
    )


def total_kernel(
    bulk_n, group_n, divisor, gram, test, sketch,
    near, far, whole, full, send_a, recv_a, send_b, recv_b, send_c, recv_c,
):
    parts, height, snaps = gram.shape
    depth = bulk_n // NEAR
    b, g = lax.axis_index("bulk"), lax.axis_index("group")
    z, q = b // NEAR, lax.rem(b, NEAR) * group_n + g

    def in_plane(d):
        other = lax.rem(q + d, parts)
        return other, (z * NEAR + other // group_n, lax.rem(other, group_n))

    def along_z(d):
        other = lax.rem(z + d, depth)
        return other, (other * NEAR + lax.rem(b, NEAR), g)

    barrier = pltpu.get_barrier_semaphore()

    def greet(where):
        def body(d, carry):
            _, peer = where(d)
            pl.semaphore_signal(barrier, inc=1, device_id=peer, device_id_type=MESH)
            return carry
        return body

    lax.fori_loop(1, parts, greet(in_plane), 0)
    lax.fori_loop(1, depth, greet(along_z), 0)
    near[pl.ds(q, 1)] = gram[pl.ds(q, 1)]
    pl.semaphore_wait(barrier, parts + depth - 2)

    def scatter(d):
        other, peer = in_plane(d)
        return pltpu.make_async_remote_copy(
            src_ref=gram.at[other], dst_ref=near.at[q], send_sem=send_a.at[d], recv_sem=recv_a.at[d],
            device_id=peer, device_id_type=MESH,
        )

    def spread(d):
        _, peer = along_z(d)
        return pltpu.make_async_remote_copy(
            src_ref=far.at[z], dst_ref=far.at[z], send_sem=send_b.at[d], recv_sem=recv_b.at[d],
            device_id=peer, device_id_type=MESH,
        )

    def gather(d):
        _, peer = in_plane(d)
        return pltpu.make_async_remote_copy(
            src_ref=whole.at[q], dst_ref=whole.at[q], send_sem=send_c.at[d], recv_sem=recv_c.at[d],
            device_id=peer, device_id_type=MESH,
        )

    def start(make):
        def body(d, carry):
            make(d).start()
            return carry
        return body

    def arrive(make):
        def body(d, carry):
            make(d).wait_recv()
            return carry
        return body

    def leave(make):
        def body(d, carry):
            make(d).wait_send()
            return carry
        return body

    lax.fori_loop(1, parts, start(scatter), 0)
    lax.fori_loop(1, parts, arrive(scatter), 0)
    far[pl.ds(z, 1)] = jnp.sum(near[...], axis=0, keepdims=True)
    lax.fori_loop(1, depth, start(spread), 0)
    lax.fori_loop(1, depth, arrive(spread), 0)
    whole[pl.ds(q, 1)] = jnp.sum(far[...], axis=0, keepdims=True)
    lax.fori_loop(1, parts, start(gather), 0)
    lax.fori_loop(1, parts, arrive(gather), 0)
    for p in range(parts):
        full[p * height : (p + 1) * height, :] = whole[p]
    sketch[...] = (
        jnp.dot(
            full[...], test[...].astype(jnp.float32),
            precision=lax.Precision.HIGHEST, preferred_element_type=jnp.float32,
        )
        / divisor
    )
    lax.fori_loop(1, parts, leave(scatter), 0)
    lax.fori_loop(1, depth, leave(spread), 0)
    lax.fori_loop(1, parts, leave(gather), 0)


def summed_sketch(gram, test, divisor, bulk_n, group_n):
    parts, height, snaps = gram.shape
    depth = bulk_n // NEAR
    width = test.shape[1]
    vmem = pl.BlockSpec(memory_space=pltpu.VMEM)
    return pl.pallas_call(
        functools.partial(total_kernel, bulk_n, group_n, divisor),
        out_shape=jax.ShapeDtypeStruct((snaps, width), jnp.float32),
        in_specs=[vmem, vmem],
        out_specs=vmem,
        scratch_shapes=[
            pltpu.VMEM((parts, height, snaps), jnp.float32),
            pltpu.VMEM((depth, height, snaps), jnp.float32),
            pltpu.VMEM((parts, height, snaps), jnp.float32),
            pltpu.VMEM((snaps, snaps), jnp.float32),
            pltpu.SemaphoreType.DMA((parts,)),
            pltpu.SemaphoreType.DMA((parts,)),
            pltpu.SemaphoreType.DMA((depth,)),
            pltpu.SemaphoreType.DMA((depth,)),
            pltpu.SemaphoreType.DMA((parts,)),
            pltpu.SemaphoreType.DMA((parts,)),
        ],
        compiler_params=pltpu.CompilerParams(
            collective_id=1, has_side_effects=True, vmem_limit_bytes=16 * MIB
        ),
        name="gram_total",
    )(gram, test)


def on_device(
    bulk_n, group_n,
    snapshots, owned_rows, iface_lists, block_columns, block_types, block_scales, mass_table, sketch_matrix,
):
    ghosts = exchanged(snapshots, iface_lists, bulk_n, group_n)
    projected, gram = mass_product(
        owned_rows, block_columns, block_types, block_scales,
        snapshots, ghosts, mass_table, sketch_matrix, bulk_n, NEAR * group_n,
    )
    sketch = summed_sketch(gram, sketch_matrix, snapshots.shape[0], bulk_n, group_n)
    return projected, sketch


def solution(mesh):
    return jax.shard_map(
        functools.partial(on_device, mesh.shape["bulk"], mesh.shape["group"]),
        mesh=mesh,
        in_specs=(
            P(("bulk", "group"), None),
            P(("bulk", "group")),
            P(("bulk", "group"), None, None),
            P(("bulk", "group"), None),
            P(("bulk", "group"), None),
            P(("bulk", "group"), None),
            P(),
            P(),
        ),
        out_specs=(P(("bulk", "group"), None), P()),
        check_vma=False,
    )
```

```python
import functools

import jax
import jax.numpy as jnp
from jax import lax
from jax.experimental import pallas as pl
from jax.experimental.pallas import tpu as pltpu
from jax.sharding import PartitionSpec as P

MESH = pl.DeviceIdType.MESH
NEAR = 2
GRANT = 64 << 20
CHUNKS = 4


def rows_kernel(
    bulk_n, group_n, lists, snap_hbm, ghosts, snap, wide, picked, packed, load_sem, send_sem, recv_sem
):
    row_count = snap.shape[0]
    faces = packed.shape[1]
    b, g = lax.axis_index("bulk"), lax.axis_index("group")
    above, below = lax.rem(b + 1, bulk_n), lax.rem(b + bulk_n - 1, bulk_n)
    right, left = lax.rem(g + 1, group_n), lax.rem(g + group_n - 1, group_n)
    plan = ((1, (above, g)), (0, (below, g)), (3, (b, right)), (2, (b, left)))

    chunk = row_count // CHUNKS
    loads = [
        pltpu.make_async_copy(snap_hbm.at[rows], snap.at[rows], load_sem.at[n])
        for n, rows in enumerate(pl.ds(i * chunk, chunk) for i in range(CHUNKS))
    ]
    for load in loads:
        load.start()
    barrier = pltpu.get_barrier_semaphore()
    for _, peer in plan:
        pl.semaphore_signal(barrier, inc=1, device_id=peer, device_id_type=MESH)
    step = 128

    def widen(i, carry):
        rows = pl.ds(pl.multiple_of(i * step, step), step)
        wide[rows, :] = snap[rows, :].astype(jnp.float32)
        return carry

    for n, load in enumerate(loads):
        load.wait()
        lax.fori_loop(n * chunk // step, (n + 1) * chunk // step, widen, 0)
    pl.semaphore_wait(barrier, len(plan))

    copies = []
    for slot, (which, peer) in enumerate(plan):

        def pick(i, carry):
            for u in range(16):
                r = i * 16 + u
                picked[pl.ds(r, 1), :] = wide[pl.ds(lists[0, which, r], 1), :]
            return carry

        lax.fori_loop(0, faces // 16, pick, 0)
        packed[slot] = picked[...].astype(jnp.bfloat16)
        copy = pltpu.make_async_remote_copy(
            src_ref=packed.at[slot],
            dst_ref=ghosts.at[slot],
            send_sem=send_sem.at[slot],
            recv_sem=recv_sem.at[slot],
            device_id=peer,
            device_id_type=MESH,
        )
        copy.start()
        copies.append(copy)
    for copy in copies:
        copy.wait()


def exchanged(snapshots, iface_lists, bulk_n, group_n):
    rows, snaps = snapshots.shape
    faces = iface_lists.shape[2]
    return pl.pallas_call(
        functools.partial(rows_kernel, bulk_n, group_n),
        out_shape=jax.ShapeDtypeStruct((4, faces, snaps), jnp.bfloat16),
        in_specs=[pl.BlockSpec(memory_space=pltpu.SMEM), pl.BlockSpec(memory_space=pl.ANY)],
        out_specs=pl.BlockSpec(memory_space=pl.ANY),
        scratch_shapes=[
            pltpu.VMEM((rows, snaps), jnp.bfloat16),
            pltpu.VMEM((rows, snaps), jnp.float32),
            pltpu.VMEM((faces, snaps), jnp.float32),
            pltpu.VMEM((4, faces, snaps), jnp.bfloat16),
            pltpu.SemaphoreType.DMA((CHUNKS,)),
            pltpu.SemaphoreType.DMA((4,)),
            pltpu.SemaphoreType.DMA((4,)),
        ],
        compiler_params=pltpu.CompilerParams(
            collective_id=0, has_side_effects=True, vmem_limit_bytes=GRANT
        ),
        name="ghost_rows",
    )(iface_lists, snapshots)


def mass_kernel(
    edges, entries, owned, columns, types, scales, snap, ghosts, table, test,
    projected, gram, cols, pairs, weighted, total,
):
    step, steps = pl.program_id(0), pl.num_programs(0)
    own, block, snaps = snap.shape
    outer = ghosts.shape[0]
    per_step = projected.shape[0] // block
    lane = lax.broadcasted_iota(jnp.int32, (1, 2 * block), 1) < block
    line = lax.broadcasted_iota(jnp.int32, (block, snaps), 0)
    count = owned[0]

    @pl.when(step == 0)
    def _():
        b = lax.axis_index("bulk")
        total[...] = jnp.zeros_like(total)
        for t in range(table.shape[0]):
            both = table[t].astype(jnp.float32)
            pairs[t] = jnp.concatenate([both, both], axis=1)

        def own_blocks(i, carry):
            keep = line + i * block < count
            cols[i] = jnp.where(keep, snap[i].astype(jnp.float32), 0.0).astype(jnp.bfloat16)
            return carry

        def ghost_blocks(i, carry):
            side = i // (outer // 4)
            gone = ((side == 0) & (b == 0)) | ((side == 1) & (b == edges - 1))
            value = ghosts[i].astype(jnp.float32)
            keep = line < jnp.where(gone, 0, block)
            cols[own + i] = jnp.where(keep, value, 0.0).astype(jnp.bfloat16)
            return carry

        lax.fori_loop(0, own, own_blocks, 0)
        lax.fori_loop(0, outer, ghost_blocks, 0)

    for u in range(per_step):
        r = step * per_step + u
        tiles = []
        for k in range(0, entries - 1, 2):
            one, two = pairs[types[k, r]], pairs[types[k + 1, r]]
            factor = jnp.where(lane, scales[k, r], scales[k + 1, r])
            tiles.append((jnp.where(lane, one, two) * factor).astype(jnp.bfloat16))
        if entries % 2:
            last = pairs[types[entries - 1, r]][:, :block] * scales[entries - 1, r]
            tiles.append(last.astype(jnp.bfloat16))
        stacked = jnp.concatenate([cols[columns[k, r]] for k in range(entries)], axis=0)
        value = jnp.dot(
            jnp.concatenate(tiles, axis=1), stacked, preferred_element_type=jnp.float32
        )
        keep = line + r * block < count
        weighted[u * block : (u + 1) * block, :] = jnp.where(keep, value, 0.0).astype(jnp.bfloat16)

    here = weighted[...]
    projected[...] = jnp.dot(here, test[...], preferred_element_type=jnp.float32).astype(jnp.bfloat16)
    mine = snap[pl.ds(step * per_step, per_step)].reshape(per_step * block, snaps)
    total[...] += lax.dot_general(
        mine, here, (((0,), (0,)), ((), ())), preferred_element_type=jnp.float32
    )

    @pl.when(step == steps - 1)
    def _():
        parts, height = gram.shape[0], gram.shape[1]
        for p in range(parts):
            gram[p] = total[p * height : (p + 1) * height, :]


def mass_product(owned, columns, types, scales, snapshots, ghosts, table, test, edges, parts):
    rows, snaps = snapshots.shape
    kinds, block, _ = table.shape
    own, outer = rows // block, ghosts.shape[0] * ghosts.shape[1] // block
    entries = columns.shape[1]
    width = test.shape[1]
    per_step = 8
    whole = lambda shape: pl.BlockSpec(shape, lambda i: (0,) * len(shape))
    scalar = pl.BlockSpec(memory_space=pltpu.SMEM)
    return pl.pallas_call(
        functools.partial(mass_kernel, edges, entries),
        grid=(own // per_step,),
        out_shape=(
            jax.ShapeDtypeStruct((rows, width), jnp.bfloat16),
            jax.ShapeDtypeStruct((parts, snaps // parts, snaps), jnp.float32),
        ),
        in_specs=[
            scalar, scalar, scalar, scalar,
            whole((own, block, snaps)),
            whole((outer, block, snaps)),
            whole((kinds, block, block)),
            whole((snaps, width)),
        ],
        out_specs=(
            pl.BlockSpec((per_step * block, width), lambda i: (i, 0)),
            whole((parts, snaps // parts, snaps)),
        ),
        scratch_shapes=[
            pltpu.VMEM((own + outer, block, snaps), jnp.bfloat16),
            pltpu.VMEM((kinds, block, 2 * block), jnp.float32),
            pltpu.VMEM((per_step * block, snaps), jnp.bfloat16),
            pltpu.VMEM((snaps, snaps), jnp.float32),
        ],
        compiler_params=pltpu.CompilerParams(vmem_limit_bytes=GRANT),
        name="mass_product",
    )(
        owned, columns.T, types.T, scales.T,
        snapshots.reshape(own, block, snaps),
        ghosts.reshape(outer, block, snaps),
        table, test,
    )


def wrapped(index, count):
    return jnp.where(index >= count, index - count, index)


def total_kernel(
    bulk_n, group_n, divisor, gram, test, sketch, near, far, whole, full, send_sem, recv_sem
):
    parts, height, snaps = gram.shape
    depth = bulk_n // NEAR
    b, g = lax.axis_index("bulk"), lax.axis_index("group")
    z, y = b // NEAR, lax.rem(b, NEAR)
    q = y * group_n + g

    def in_plane(d):
        other = wrapped(q + d, parts)
        up = sum((other >= n * group_n).astype(jnp.int32) for n in range(1, NEAR))
        return other, (z * NEAR + up, other - up * group_n)

    def along_z(d):
        other = wrapped(z + d, depth)
        return other, (other * NEAR + y, g)

    barrier = pltpu.get_barrier_semaphore()
    for where, count in ((in_plane, parts), (along_z, depth)):
        for d in range(1, count):
            pl.semaphore_signal(barrier, inc=1, device_id=where(d)[1], device_id_type=MESH)
    near[pl.ds(q, 1)] = gram[pl.ds(q, 1)]
    pl.semaphore_wait(barrier, parts + depth - 2)

    def copy(phase, source, target, peer):
        return pltpu.make_async_remote_copy(
            src_ref=source, dst_ref=target, send_sem=send_sem.at[phase], recv_sem=recv_sem.at[phase],
            device_id=peer, device_id_type=MESH,
        )

    def all_of(phase, buffer):
        some = buffer.at[pl.ds(0, buffer.shape[0] - 1)]
        return copy(phase, some, some, (b, g))

    for d in range(1, parts):
        other, peer = in_plane(d)
        copy(0, gram.at[other], near.at[q], peer).start()
    all_of(0, near).wait_recv()
    far[pl.ds(z, 1)] = jnp.sum(near[...], axis=0, keepdims=True)
    for d in range(1, depth):
        copy(1, far.at[z], far.at[z], along_z(d)[1]).start()
    all_of(1, far).wait_recv()
    whole[pl.ds(q, 1)] = jnp.sum(far[...], axis=0, keepdims=True)
    for d in range(1, parts):
        copy(2, whole.at[q], whole.at[q], in_plane(d)[1]).start()
    all_of(2, whole).wait_recv()
    for p in range(parts):
        full[p * height : (p + 1) * height, :] = whole[p]
    sketch[...] = (
        jnp.dot(
            full[...], test[...].astype(jnp.float32),
            precision=lax.Precision.HIGHEST, preferred_element_type=jnp.float32,
        )
        / divisor
    )
    all_of(0, near).wait_send()
    all_of(1, far).wait_send()
    all_of(2, whole).wait_send()


def summed_sketch(gram, test, divisor, bulk_n, group_n):
    parts, height, snaps = gram.shape
    depth = bulk_n // NEAR
    width = test.shape[1]
    vmem = pl.BlockSpec(memory_space=pltpu.VMEM)
    return pl.pallas_call(
        functools.partial(total_kernel, bulk_n, group_n, divisor),
        out_shape=jax.ShapeDtypeStruct((snaps, width), jnp.float32),
        in_specs=[vmem, vmem],
        out_specs=vmem,
        scratch_shapes=[
            pltpu.VMEM((parts, height, snaps), jnp.float32),
            pltpu.VMEM((depth, height, snaps), jnp.float32),
            pltpu.VMEM((parts, height, snaps), jnp.float32),
            pltpu.VMEM((snaps, snaps), jnp.float32),
            pltpu.SemaphoreType.DMA((3,)),
            pltpu.SemaphoreType.DMA((3,)),
        ],
        compiler_params=pltpu.CompilerParams(
            collective_id=1, has_side_effects=True, vmem_limit_bytes=GRANT
        ),
        name="gram_total",
    )(gram, test)


def on_device(
    bulk_n, group_n,
    snapshots, owned_rows, iface_lists, block_columns, block_types, block_scales, mass_table, sketch_matrix,
):
    ghosts = exchanged(snapshots, iface_lists, bulk_n, group_n)
    projected, gram = mass_product(
        owned_rows, block_columns, block_types, block_scales,
        snapshots, ghosts, mass_table, sketch_matrix, bulk_n, NEAR * group_n,
    )
    sketch = summed_sketch(gram, sketch_matrix, snapshots.shape[0], bulk_n, group_n)
    return projected, sketch


def solution(mesh):
    return jax.shard_map(
        functools.partial(on_device, mesh.shape["bulk"], mesh.shape["group"]),
        mesh=mesh,
        in_specs=(
            P(("bulk", "group"), None),
            P(("bulk", "group")),
            P(("bulk", "group"), None, None),
            P(("bulk", "group"), None),
            P(("bulk", "group"), None),
            P(("bulk", "group"), None),
            P(),
            P(),
        ),
        out_specs=(P(("bulk", "group"), None), P()),
        check_vma=False,
    )
```

```python
import functools

import jax
import jax.numpy as jnp
from jax import lax
from jax.experimental import pallas as pl
from jax.experimental.pallas import tpu as pltpu
from jax.sharding import PartitionSpec as P

MESH = pl.DeviceIdType.MESH
NEAR = 2
GRANT = 64 << 20
PIECES = 12
CHUNKS = 4
STEP = 8
WIDE = 4


def wrapped(index, count):
    return jnp.where(index >= count, index - count, index)


def partition_kernel(
    bulk_n, group_n, owned, lists_hbm, columns_hbm, types_hbm, scales_hbm, snap_hbm, table_hbm, test_hbm,
    projected_hbm, summed, lists, columns, types, scales, table, test,
    cols, wide, picked, packed, pairs, scaled, weighted, projected, total, gram, near, far,
    load_sem, late_sem, ghost_send, ghost_recv, sum_send, sum_recv, store_sem,
):
    own, block, snaps = snap_hbm.shape
    faces = picked.shape[0]
    face_blocks = faces // block
    entries = columns.shape[0]
    parts, height, _ = gram.shape
    depth = bulk_n // NEAR
    count = owned[0]
    b, g = lax.axis_index("bulk"), lax.axis_index("group")
    z, y = b // NEAR, lax.rem(b, NEAR)
    q = y * group_n + g
    line = lax.broadcasted_iota(jnp.int32, (block, snaps), 0)

    def in_plane(d):
        other = wrapped(q + d, parts)
        up = (other >= group_n).astype(jnp.int32)
        return other, (z * NEAR + up, other - up * group_n)

    def along_z(d):
        return (wrapped(z + d, depth) * NEAR + y, g)

    above, below = lax.rem(b + 1, bulk_n), lax.rem(b + bulk_n - 1, bulk_n)
    right, left = lax.rem(g + 1, group_n), lax.rem(g + group_n - 1, group_n)
    plan = ((1, (above, g)), (0, (below, g)), (3, (b, right)), (2, (b, left)))

    chunk = own // CHUNKS
    loads = [
        pltpu.make_async_copy(
            snap_hbm.at[pl.ds(n * chunk, chunk)], cols.at[pl.ds(n * chunk, chunk)], load_sem.at[n]
        )
        for n in range(CHUNKS)
    ]
    early = pltpu.make_async_copy(lists_hbm, lists, load_sem.at[CHUNKS])
    late = [
        pltpu.make_async_copy(source, target, late_sem.at[n])
        for n, (source, target) in enumerate(
            (
                (columns_hbm, columns), (types_hbm, types), (scales_hbm, scales),
                (table_hbm, table), (test_hbm, test),
            )
        )
    ]
    for load in [early] + loads + late:
        load.start()

    barrier = pltpu.get_barrier_semaphore()
    slanted = jnp.where(y == 0, below, above)
    peers = [(slanted, g)] + [in_plane(d)[1] for d in range(1, parts)]
    peers += [along_z(d) for d in range(1, depth)]
    for peer in peers:
        pl.semaphore_signal(barrier, inc=1, device_id=peer, device_id_type=MESH)

    def widen(i, carry):
        for u in range(WIDE):
            r = i * WIDE + u
            wide[pl.ds(pl.multiple_of(r * block, block), block), :] = cols[r].astype(jnp.float32)
        return carry

    for n, load in enumerate(loads):
        load.wait()
        lax.fori_loop(n * chunk // WIDE, (n + 1) * chunk // WIDE, widen, 0)

    early.wait()
    ghosts = []
    for slot, (which, peer) in enumerate(plan):

        def pick(i, carry):
            for u in range(16):
                r = i * 16 + u
                picked[pl.ds(r, 1), :] = wide[pl.ds(lists[0, which, r], 1), :]
            return carry

        lax.fori_loop(0, faces // 16, pick, 0)
        packed[slot] = picked[...].astype(jnp.bfloat16).reshape(face_blocks, block, snaps)
        copy = pltpu.make_async_remote_copy(
            src_ref=packed.at[slot],
            dst_ref=cols.at[pl.ds(own + slot * face_blocks, face_blocks)],
            send_sem=ghost_send.at[slot],
            recv_sem=ghost_recv.at[slot],
            device_id=peer,
            device_id_type=MESH,
        )
        if slot == 0:
            pl.semaphore_wait(barrier, len(peers))
        copy.start()
        ghosts.append(copy)

    for load in late:
        load.wait()
    lane = lax.broadcasted_iota(jnp.int32, (1, 2 * block), 1) < block
    for t in range(table.shape[0]):
        both = table[t].astype(jnp.float32)
        pairs[t] = jnp.concatenate([both, both], axis=1)

    def scale_row(i, carry):
        for u in range(WIDE):
            r = i * WIDE + u
            kept = line + r * block < count
            cols[r] = jnp.where(kept, cols[r].astype(jnp.float32), 0.0).astype(jnp.bfloat16)
            for k in range(0, entries - 1, 2):
                one, two = pairs[types[k, r]], pairs[types[k + 1, r]]
                factor = jnp.where(lane, scales[k, r], scales[k + 1, r])
                tile = (jnp.where(lane, one, two) * factor).astype(jnp.bfloat16)
                scaled[r, :, k * block : (k + 2) * block] = tile
            if entries % 2:
                last = pairs[types[entries - 1, r]][:, :block] * scales[entries - 1, r]
                scaled[r, :, (entries - 1) * block :] = last.astype(jnp.bfloat16)
        return carry

    lax.fori_loop(0, own // WIDE, scale_row, 0)
    total[...] = jnp.zeros_like(total)
    weighted[pl.ds(0, STEP)] = jnp.zeros((STEP, block, snaps), jnp.bfloat16)
    for copy in ghosts:
        copy.wait()
    for slot, edge in ((0, 0), (1, bulk_n - 1)):

        @pl.when(b == edge)
        def _():
            first = own + slot * face_blocks
            cols[first : first + face_blocks] = jnp.zeros((face_blocks, block, snaps), jnp.bfloat16)

    def gram_step(i):
        rows = pl.ds(i * STEP, STEP)
        total[...] += lax.dot_general(
            cols[rows].reshape(STEP * block, snaps), weighted[rows].reshape(STEP * block, snaps),
            (((0,), (0,)), ((), ())), preferred_element_type=jnp.float32,
        )

    def mass_step(i, carry):
        gram_step(jnp.maximum(i - 1, 0))
        for u in range(STEP):
            r = i * STEP + u
            stacked = jnp.concatenate([cols[columns[k, r]] for k in range(entries)], axis=0)
            value = jnp.dot(scaled[r], stacked, preferred_element_type=jnp.float32)
            keep = line + r * block < count
            weighted[r] = jnp.where(keep, value, 0.0).astype(jnp.bfloat16)
        return carry

    lax.fori_loop(0, own // STEP, mass_step, 0)
    gram_step(own // STEP - 1)

    def project(phase):
        def one(i, carry):
            here = weighted[pl.ds(i * STEP, STEP)].reshape(STEP * block, snaps)
            rows = pl.ds(pl.multiple_of(i * (STEP * block), STEP * block), STEP * block)
            product = jnp.dot(here, test[...], preferred_element_type=jnp.float32)
            projected[rows, :] = product.astype(jnp.bfloat16)
            return carry

        steps = own // STEP
        first, last = phase * steps // 3, (phase + 1) * steps // 3
        lax.fori_loop(first, last, one, 0)
        rows = pl.ds(first * STEP * block, (last - first) * STEP * block)
        store = pltpu.make_async_copy(projected.at[rows], projected_hbm.at[rows], store_sem.at[phase])
        store.start()
        return store

    for p in range(parts):
        gram[p] = total[p * height : (p + 1) * height, :]
    near[pl.ds(q, 1)] = gram[pl.ds(q, 1)]

    def copy(phase, source, target, peer):
        return pltpu.make_async_remote_copy(
            src_ref=source, dst_ref=target, send_sem=sum_send.at[phase], recv_sem=sum_recv.at[phase],
            device_id=peer, device_id_type=MESH,
        )

    def all_of(phase, buffer):
        some = buffer.at[pl.ds(0, buffer.shape[0] - 1)]
        return copy(phase, some, some, (b, g))

    for d in range(1, parts):
        other, peer = in_plane(d)
        copy(0, gram.at[other], near.at[q], peer).start()
    stores = [project(0)]
    all_of(0, near).wait_recv()
    far[pl.ds(z, 1)] = jnp.sum(near[...], axis=0, keepdims=True)
    for d in sorted(range(1, depth), key=lambda d: -min(d, depth - d)):
        copy(1, far.at[z], far.at[z], along_z(d)).start()
    stores.append(project(1))
    all_of(1, far).wait_recv()
    summed[pl.ds(q, 1)] = jnp.sum(far[...], axis=0, keepdims=True)
    for d in range(1, parts):
        copy(2, summed.at[q], summed.at[q], in_plane(d)[1]).start()
    stores.append(project(2))
    all_of(2, summed).wait_recv()
    all_of(0, near).wait_send()
    all_of(1, far).wait_send()
    all_of(2, summed).wait_send()
    for store in stores:
        store.wait()


def partition_terms(
    snapshots, owned, lists, columns, types, scales, table, test, bulk_n, group_n
):
    rows, snaps = snapshots.shape
    kinds, block, _ = table.shape
    own, entries = columns.shape
    faces = lists.shape[2]
    outer = 4 * faces // block
    parts, depth = NEAR * group_n, bulk_n // NEAR
    height = snaps // parts
    scalar = pl.BlockSpec(memory_space=pltpu.SMEM)
    vmem = pl.BlockSpec(memory_space=pltpu.VMEM)
    return pl.pallas_call(
        functools.partial(partition_kernel, bulk_n, group_n),
        out_shape=(
            jax.ShapeDtypeStruct((rows, test.shape[1]), jnp.bfloat16),
            jax.ShapeDtypeStruct((parts, height, snaps), jnp.float32),
        ),
        in_specs=[scalar] + [pl.BlockSpec(memory_space=pl.ANY)] * 7,
        out_specs=(pl.BlockSpec(memory_space=pl.ANY), vmem),
        scratch_shapes=[
            pltpu.SMEM(lists.shape, jnp.int32),
            pltpu.SMEM((entries, own), jnp.int32),
            pltpu.SMEM((entries, own), jnp.int32),
            pltpu.SMEM((entries, own), jnp.float32),
            pltpu.VMEM(table.shape, table.dtype),
            pltpu.VMEM(test.shape, test.dtype),
            pltpu.VMEM((own + outer, block, snaps), jnp.bfloat16),
            pltpu.VMEM((rows, snaps), jnp.float32),
            pltpu.VMEM((faces, snaps), jnp.float32),
            pltpu.VMEM((4, faces // block, block, snaps), jnp.bfloat16),
            pltpu.VMEM((kinds, block, 2 * block), jnp.float32),
            pltpu.VMEM((own, block, entries * block), jnp.bfloat16),
            pltpu.VMEM((own, block, snaps), jnp.bfloat16),
            pltpu.VMEM((rows, test.shape[1]), jnp.bfloat16),
            pltpu.VMEM((snaps, snaps), jnp.float32),
            pltpu.VMEM((parts, height, snaps), jnp.float32),
            pltpu.VMEM((parts, height, snaps), jnp.float32),
            pltpu.VMEM((depth, height, snaps), jnp.float32),
            pltpu.SemaphoreType.DMA((CHUNKS + 1,)),
            pltpu.SemaphoreType.DMA((5,)),
            pltpu.SemaphoreType.DMA((4,)),
            pltpu.SemaphoreType.DMA((4,)),
            pltpu.SemaphoreType.DMA((3,)),
            pltpu.SemaphoreType.DMA((3,)),
            pltpu.SemaphoreType.DMA((3,)),
        ],
        compiler_params=pltpu.CompilerParams(
            collective_id=0, has_side_effects=True, vmem_limit_bytes=GRANT
        ),
        name="partition_terms",
    )(owned, lists, columns.T, types.T, scales.T, snapshots.reshape(own, block, snaps), table, test)


def outputs_kernel(divisor, made, summed_hbm, test_hbm, projected, sketch_hbm, held, summed, test, full, sketch, sems, out_sems):
    small = [
        pltpu.make_async_copy(summed_hbm, summed, sems.at[PIECES]),
        pltpu.make_async_copy(test_hbm, test, sems.at[PIECES + 1]),
    ]
    size = made.shape[0] // PIECES
    pieces = [pl.ds(n * size, size) for n in range(PIECES)]
    loads = [pltpu.make_async_copy(made.at[p], held.at[p], sems.at[n]) for n, p in enumerate(pieces)]
    stores = [pltpu.make_async_copy(held.at[p], projected.at[p], out_sems.at[n]) for n, p in enumerate(pieces)]
    for copy in small + loads:
        copy.start()
    for load, store in zip(loads, stores):
        load.wait()
        store.start()
    for copy in small:
        copy.wait()
    parts, height, _ = summed.shape
    for p in range(parts):
        full[p * height : (p + 1) * height, :] = summed[p]
    product = jnp.dot(
        full[...], test[...].astype(jnp.float32),
        precision=lax.Precision.HIGHEST, preferred_element_type=jnp.float32,
    )
    sketch[...] = product / divisor
    last = pltpu.make_async_copy(sketch, sketch_hbm, sems.at[PIECES + 2])
    last.start()
    for copy in stores + [last]:
        copy.wait()


def final_outputs(made, summed, test):
    rows, width = made.shape
    snaps = test.shape[0]
    anywhere = pl.BlockSpec(memory_space=pl.ANY)
    return pl.pallas_call(
        functools.partial(outputs_kernel, rows),
        out_shape=(
            jax.ShapeDtypeStruct((rows, width), jnp.bfloat16),
            jax.ShapeDtypeStruct((snaps, width), jnp.float32),
        ),
        in_specs=[anywhere] * 3,
        out_specs=(anywhere, anywhere),
        scratch_shapes=[
            pltpu.VMEM(made.shape, made.dtype),
            pltpu.VMEM(summed.shape, jnp.float32),
            pltpu.VMEM(test.shape, jnp.bfloat16),
            pltpu.VMEM((snaps, snaps), jnp.float32),
            pltpu.VMEM((snaps, width), jnp.float32),
            pltpu.SemaphoreType.DMA((PIECES + 3,)),
            pltpu.SemaphoreType.DMA((PIECES,)),
        ],
        compiler_params=pltpu.CompilerParams(vmem_limit_bytes=GRANT),
        name="final_outputs",
    )(made, summed, test)


def on_device(
    bulk_n, group_n,
    snapshots, owned_rows, iface_lists, block_columns, block_types, block_scales, mass_table, sketch_matrix,
):
    made, summed = partition_terms(
        snapshots, owned_rows, iface_lists, block_columns, block_types, block_scales, mass_table,
        sketch_matrix, bulk_n, group_n,
    )
    return final_outputs(made, summed, sketch_matrix)


def solution(mesh):
    return jax.shard_map(
        functools.partial(on_device, mesh.shape["bulk"], mesh.shape["group"]),
        mesh=mesh,
        in_specs=(
            P(("bulk", "group"), None),
            P(("bulk", "group")),
            P(("bulk", "group"), None, None),
            P(("bulk", "group"), None),
            P(("bulk", "group"), None),
            P(("bulk", "group"), None),
            P(),
            P(),
        ),
        out_specs=(P(("bulk", "group"), None), P()),
        check_vma=False,
    )
```

```python
import functools

import jax
import jax.numpy as jnp
from jax import lax
from jax.experimental import pallas as pl
from jax.experimental.pallas import tpu as pltpu
from jax.sharding import PartitionSpec as P

MESH = pl.DeviceIdType.MESH
NEAR = 2
GRANT = 64 << 20
ROOM = 16 << 20
PIECES = 12
CHUNKS = 4
HALVES = 2
STEP = 16
WIDE = 4


def wrapped(index, count):
    return jnp.where(index >= count, index - count, index)


def partition_kernel(
    bulk_n, group_n, owned, lists_hbm, columns_hbm, types_hbm, scales_hbm, snap_hbm, table_hbm, test_hbm,
    projected, summed, lists, columns, types, scales, table, test,
    cols, wide, picked, packed, pairs, scaled, weighted, total, gram, near, far,
    load_sem, late_sem, ghost_send, ghost_recv, sum_send, sum_recv,
):
    own, block, snaps = snap_hbm.shape
    face_blocks = packed.shape[1]
    entries = columns.shape[0]
    parts, height, _ = gram.shape
    depth = bulk_n // NEAR
    count = owned[0]
    b, g = lax.axis_index("bulk"), lax.axis_index("group")
    z, y = b // NEAR, lax.rem(b, NEAR)
    q = y * group_n + g
    line = lax.broadcasted_iota(jnp.int32, (block, snaps), 0)

    def in_plane(d):
        other = wrapped(q + d, parts)
        up = (other >= group_n).astype(jnp.int32)
        return other, (z * NEAR + up, other - up * group_n)

    def along_z(d):
        return (wrapped(z + d, depth) * NEAR + y, g)

    above, below = lax.rem(b + 1, bulk_n), lax.rem(b + bulk_n - 1, bulk_n)
    right, left = lax.rem(g + 1, group_n), lax.rem(g + group_n - 1, group_n)
    plan = ((1, (above, g)), (0, (below, g)), (3, (b, right)), (2, (b, left)))

    chunk = own // CHUNKS
    loads = [
        pltpu.make_async_copy(
            snap_hbm.at[pl.ds(n * chunk, chunk)], cols.at[pl.ds(n * chunk, chunk)], load_sem.at[n]
        )
        for n in range(CHUNKS)
    ]
    early = pltpu.make_async_copy(lists_hbm, lists, load_sem.at[CHUNKS])
    late = [
        pltpu.make_async_copy(source, target, late_sem.at[n])
        for n, (source, target) in enumerate(
            (
                (columns_hbm, columns), (types_hbm, types), (scales_hbm, scales),
                (table_hbm, table), (test_hbm, test),
            )
        )
    ]
    for load in [early] + loads + late:
        load.start()

    barrier = pltpu.get_barrier_semaphore()
    slanted = jnp.where(y == 0, below, above)
    peers = [(slanted, g)] + [in_plane(d)[1] for d in range(1, parts)]
    peers += [along_z(d) for d in range(1, depth)]
    for peer in peers:
        pl.semaphore_signal(barrier, inc=1, device_id=peer, device_id_type=MESH)

    def widen(i, carry):
        for u in range(WIDE):
            r = i * WIDE + u
            wide[pl.ds(pl.multiple_of(r * block, block), block), :] = cols[r].astype(jnp.float32)
        return carry

    for n, load in enumerate(loads):
        load.wait()
        lax.fori_loop(n * chunk // WIDE, (n + 1) * chunk // WIDE, widen, 0)

    early.wait()
    ghosts = []
    half = face_blocks // HALVES
    for slot, (which, peer) in enumerate(plan):
        for part in range(HALVES):
            base = part * half * block

            def pick(i, carry):
                for u in range(16):
                    r = i * 16 + u
                    picked[pl.ds(r, 1), :] = wide[pl.ds(lists[0, which, base + r], 1), :]
                return carry

            lax.fori_loop(0, half * block // 16, pick, 0)
            rows = pl.ds(part * half, half)
            packed[slot, rows] = picked[...].astype(jnp.bfloat16).reshape(half, block, snaps)
            number = slot * HALVES + part
            copy = pltpu.make_async_remote_copy(
                src_ref=packed.at[slot, rows],
                dst_ref=cols.at[pl.ds(own + number * half, half)],
                send_sem=ghost_send.at[number],
                recv_sem=ghost_recv.at[number],
                device_id=peer,
                device_id_type=MESH,
            )
            if number == 0:
                pl.semaphore_wait(barrier, len(peers))
            copy.start()
            ghosts.append(copy)

    for load in late:
        load.wait()
    lane = lax.broadcasted_iota(jnp.int32, (1, 2 * block), 1) < block
    for t in range(table.shape[0]):
        both = table[t].astype(jnp.float32)
        pairs[t] = jnp.concatenate([both, both], axis=1)

    def scale_row(i, carry):
        for u in range(WIDE):
            r = i * WIDE + u
            kept = line + r * block < count
            cols[r] = jnp.where(kept, cols[r].astype(jnp.float32), 0.0).astype(jnp.bfloat16)
            for k in range(0, entries - 1, 2):
                one, two = pairs[types[k, r]], pairs[types[k + 1, r]]
                factor = jnp.where(lane, scales[k, r], scales[k + 1, r])
                tile = (jnp.where(lane, one, two) * factor).astype(jnp.bfloat16)
                scaled[r, :, k * block : (k + 2) * block] = tile
            if entries % 2:
                last = pairs[types[entries - 1, r]][:, :block] * scales[entries - 1, r]
                scaled[r, :, (entries - 1) * block :] = last.astype(jnp.bfloat16)
        return carry

    lax.fori_loop(0, own // WIDE, scale_row, 0)
    total[...] = jnp.zeros_like(total)
    weighted[pl.ds(0, STEP)] = jnp.zeros((STEP, block, snaps), jnp.bfloat16)
    for copy in ghosts:
        copy.wait()
    for slot, edge in ((0, 0), (1, bulk_n - 1)):

        @pl.when(b == edge)
        def _():
            first = own + slot * face_blocks
            cols[first : first + face_blocks] = jnp.zeros((face_blocks, block, snaps), jnp.bfloat16)

    def gram_step(i):
        rows = pl.ds(i * STEP, STEP)
        total[...] += lax.dot_general(
            cols[rows].reshape(STEP * block, snaps), weighted[rows].reshape(STEP * block, snaps),
            (((0,), (0,)), ((), ())), preferred_element_type=jnp.float32,
        )

    def mass_step(i, carry):
        gram_step(jnp.maximum(i - 1, 0))
        for u in range(STEP):
            r = i * STEP + u
            stacked = jnp.concatenate([cols[columns[k, r]] for k in range(entries)], axis=0)
            value = jnp.dot(scaled[r], stacked, preferred_element_type=jnp.float32)
            keep = line + r * block < count
            weighted[r] = jnp.where(keep, value, 0.0).astype(jnp.bfloat16)
        return carry

    lax.fori_loop(0, own // STEP, mass_step, 0)
    gram_step(own // STEP - 1)

    def project(phase):
        def one(i, carry):
            here = weighted[pl.ds(i * STEP, STEP)].reshape(STEP * block, snaps)
            rows = pl.ds(pl.multiple_of(i * (STEP * block), STEP * block), STEP * block)
            product = jnp.dot(here, test[...], preferred_element_type=jnp.float32)
            projected[rows, :] = product.astype(jnp.bfloat16)
            return carry

        steps = own // STEP
        first, last = phase * steps // 3, (phase + 1) * steps // 3
        lax.fori_loop(first, last, one, 0)

    for p in range(parts):
        gram[p] = total[p * height : (p + 1) * height, :]
    near[pl.ds(q, 1)] = gram[pl.ds(q, 1)]

    def copy(phase, source, target, peer):
        return pltpu.make_async_remote_copy(
            src_ref=source, dst_ref=target, send_sem=sum_send.at[phase], recv_sem=sum_recv.at[phase],
            device_id=peer, device_id_type=MESH,
        )

    def all_of(phase, buffer):
        some = buffer.at[pl.ds(0, buffer.shape[0] - 1)]
        return copy(phase, some, some, (b, g))

    for d in range(1, parts):
        other, peer = in_plane(d)
        copy(0, gram.at[other], near.at[q], peer).start()
    project(0)
    all_of(0, near).wait_recv()
    far[pl.ds(z, 1)] = jnp.sum(near[...], axis=0, keepdims=True)
    for d in sorted(range(1, depth), key=lambda d: -min(d, depth - d)):
        copy(1, far.at[z], far.at[z], along_z(d)).start()
    project(1)
    all_of(1, far).wait_recv()
    summed[pl.ds(q, 1)] = jnp.sum(far[...], axis=0, keepdims=True)
    for d in range(1, parts):
        copy(2, summed.at[q], summed.at[q], in_plane(d)[1]).start()
    project(2)
    all_of(2, summed).wait_recv()
    all_of(0, near).wait_send()
    all_of(1, far).wait_send()
    all_of(2, summed).wait_send()


def partition_terms(
    snapshots, owned, lists, columns, types, scales, table, test, bulk_n, group_n
):
    rows, snaps = snapshots.shape
    kinds, block, _ = table.shape
    own, entries = columns.shape
    faces = lists.shape[2]
    outer = 4 * faces // block
    parts, depth = NEAR * group_n, bulk_n // NEAR
    height = snaps // parts
    scalar = pl.BlockSpec(memory_space=pltpu.SMEM)
    vmem = pl.BlockSpec(memory_space=pltpu.VMEM)
    return pl.pallas_call(
        functools.partial(partition_kernel, bulk_n, group_n),
        out_shape=(
            pltpu.VMEM((rows, test.shape[1]), jnp.bfloat16),
            pltpu.VMEM((parts, height, snaps), jnp.float32),
        ),
        in_specs=[scalar] + [pl.BlockSpec(memory_space=pltpu.HBM)] * 7,
        out_specs=(vmem, vmem),
        scratch_shapes=[
            pltpu.SMEM(lists.shape, jnp.int32),
            pltpu.SMEM((entries, own), jnp.int32),
            pltpu.SMEM((entries, own), jnp.int32),
            pltpu.SMEM((entries, own), jnp.float32),
            pltpu.VMEM(table.shape, table.dtype),
            pltpu.VMEM(test.shape, test.dtype),
            pltpu.VMEM((own + outer, block, snaps), jnp.bfloat16),
            pltpu.VMEM((rows, snaps), jnp.float32),
            pltpu.VMEM((faces // HALVES, snaps), jnp.float32),
            pltpu.VMEM((4, faces // block, block, snaps), jnp.bfloat16),
            pltpu.VMEM((kinds, block, 2 * block), jnp.float32),
            pltpu.VMEM((own, block, entries * block), jnp.bfloat16),
            pltpu.VMEM((own, block, snaps), jnp.bfloat16),
            pltpu.VMEM((snaps, snaps), jnp.float32),
            pltpu.VMEM((parts, height, snaps), jnp.float32),
            pltpu.VMEM((parts, height, snaps), jnp.float32),
            pltpu.VMEM((depth, height, snaps), jnp.float32),
            pltpu.SemaphoreType.DMA((CHUNKS + 1,)),
            pltpu.SemaphoreType.DMA((5,)),
            pltpu.SemaphoreType.DMA((4 * HALVES,)),
            pltpu.SemaphoreType.DMA((4 * HALVES,)),
            pltpu.SemaphoreType.DMA((3,)),
            pltpu.SemaphoreType.DMA((3,)),
        ],
        compiler_params=pltpu.CompilerParams(
            collective_id=0, has_side_effects=True, vmem_limit_bytes=GRANT - ROOM
        ),
        name="partition_terms",
    )(
        owned,
        *(
            pltpu.with_memory_space_constraint(x, pltpu.HBM)
            for x in (
                lists, columns.T, types.T, scales.T, snapshots.reshape(own, block, snaps), table, test,
            )
        ),
    )


def outputs_kernel(divisor, made, summed, test_hbm, projected, sketch_hbm, test, full, sketch, sems):
    size = made.shape[0] // PIECES
    pieces = [pl.ds(n * size, size) for n in range(PIECES)]
    load = pltpu.make_async_copy(test_hbm, test, sems.at[PIECES])
    stores = [pltpu.make_async_copy(made.at[p], projected.at[p], sems.at[n]) for n, p in enumerate(pieces)]
    for copy in [load] + stores:
        copy.start()
    load.wait()
    parts, height, _ = summed.shape
    for p in range(parts):
        full[p * height : (p + 1) * height, :] = summed[p]
    product = jnp.dot(
        full[...], test[...].astype(jnp.float32),
        precision=lax.Precision.HIGHEST, preferred_element_type=jnp.float32,
    )
    sketch[...] = product / divisor
    last = pltpu.make_async_copy(sketch, sketch_hbm, sems.at[PIECES + 1])
    last.start()
    for copy in stores + [last]:
        copy.wait()


def final_outputs(made, summed, test):
    rows, width = made.shape
    snaps = test.shape[0]
    anywhere = pl.BlockSpec(memory_space=pltpu.HBM)
    vmem = pl.BlockSpec(memory_space=pltpu.VMEM)
    return pl.pallas_call(
        functools.partial(outputs_kernel, rows),
        out_shape=(
            jax.ShapeDtypeStruct((rows, width), jnp.bfloat16),
            jax.ShapeDtypeStruct((snaps, width), jnp.float32),
        ),
        in_specs=[vmem, vmem, anywhere],
        out_specs=(anywhere, anywhere),
        scratch_shapes=[
            pltpu.VMEM(test.shape, jnp.bfloat16),
            pltpu.VMEM((snaps, snaps), jnp.float32),
            pltpu.VMEM((snaps, width), jnp.float32),
            pltpu.SemaphoreType.DMA((PIECES + 2,)),
        ],
        compiler_params=pltpu.CompilerParams(vmem_limit_bytes=GRANT - ROOM),
        name="final_outputs",
    )(made, summed, pltpu.with_memory_space_constraint(test, pltpu.HBM))


def on_device(
    bulk_n, group_n,
    snapshots, owned_rows, iface_lists, block_columns, block_types, block_scales, mass_table, sketch_matrix,
):
    made, summed = partition_terms(
        snapshots, owned_rows, iface_lists, block_columns, block_types, block_scales, mass_table,
        sketch_matrix, bulk_n, group_n,
    )
    return final_outputs(made, summed, sketch_matrix)


def solution(mesh):
    return jax.shard_map(
        functools.partial(on_device, mesh.shape["bulk"], mesh.shape["group"]),
        mesh=mesh,
        in_specs=(
            P(("bulk", "group"), None),
            P(("bulk", "group")),
            P(("bulk", "group"), None, None),
            P(("bulk", "group"), None),
            P(("bulk", "group"), None),
            P(("bulk", "group"), None),
            P(),
            P(),
        ),
        out_specs=(P(("bulk", "group"), None), P()),
        check_vma=False,
    )
```

```python
import functools

import jax
import jax.numpy as jnp
from jax import lax
from jax.experimental import pallas as pl
from jax.experimental.pallas import tpu as pltpu
from jax.sharding import PartitionSpec as P

MESH = pl.DeviceIdType.MESH
NEAR = 2
GRANT = 64 << 20
ROOM = 16 << 20
PIECES = 12
CHUNKS = 4
HALVES = 2
STEP = 16
WIDE = 8


def wrapped(index, count):
    return jnp.where(index >= count, index - count, index)


def partition_kernel(
    bulk_n, group_n, owned, lists_hbm, columns_hbm, types_hbm, scales_hbm, snap_hbm, table_hbm, test_hbm,
    projected, summed, lists, columns, types, scales, table, test,
    cols, wide, picked, packed, pairs, scaled, weighted, total, gram, near, far,
    load_sem, late_sem, ghost_send, ghost_recv, sum_send, sum_recv,
):
    own, block, snaps = snap_hbm.shape
    face_blocks = packed.shape[1]
    entries = columns.shape[0]
    parts, height, _ = gram.shape
    depth = bulk_n // NEAR
    count = owned[0]
    b, g = lax.axis_index("bulk"), lax.axis_index("group")
    z, y = b // NEAR, lax.rem(b, NEAR)
    q = y * group_n + g
    line = lax.broadcasted_iota(jnp.int32, (block, snaps), 0)

    def in_plane(d):
        other = wrapped(q + d, parts)
        up = (other >= group_n).astype(jnp.int32)
        return other, (z * NEAR + up, other - up * group_n)

    def along_z(d):
        return (wrapped(z + d, depth) * NEAR + y, g)

    above, below = lax.rem(b + 1, bulk_n), lax.rem(b + bulk_n - 1, bulk_n)
    right, left = lax.rem(g + 1, group_n), lax.rem(g + group_n - 1, group_n)
    plan = ((1, (above, g)), (0, (below, g)), (3, (b, right)), (2, (b, left)))

    chunk = own // CHUNKS
    loads = [
        pltpu.make_async_copy(
            snap_hbm.at[pl.ds(n * chunk, chunk)], cols.at[pl.ds(n * chunk, chunk)], load_sem.at[n]
        )
        for n in range(CHUNKS)
    ]
    early = pltpu.make_async_copy(lists_hbm, lists, load_sem.at[CHUNKS])
    late = [
        pltpu.make_async_copy(source, target, late_sem.at[n])
        for n, (source, target) in enumerate(
            (
                (columns_hbm, columns), (types_hbm, types), (scales_hbm, scales),
                (table_hbm, table), (test_hbm, test),
            )
        )
    ]
    for load in [early] + loads + late:
        load.start()

    barrier = pltpu.get_barrier_semaphore()
    slanted = jnp.where(y == 0, below, above)
    peers = [(slanted, g)] + [in_plane(d)[1] for d in range(1, parts)]
    peers += [along_z(d) for d in range(1, depth)]
    for peer in peers:
        pl.semaphore_signal(barrier, inc=1, device_id=peer, device_id_type=MESH)

    def widen(i, carry):
        for u in range(WIDE):
            r = i * WIDE + u
            wide[pl.ds(pl.multiple_of(r * block, block), block), :] = cols[r].astype(jnp.float32)
        return carry

    for n, load in enumerate(loads):
        load.wait()
        lax.fori_loop(n * chunk // WIDE, (n + 1) * chunk // WIDE, widen, 0)

    early.wait()
    ghosts = []
    half = face_blocks // HALVES
    for slot, (which, peer) in enumerate(plan):
        for part in range(HALVES):
            base = part * half * block

            def pick(i, carry):
                for u in range(32):
                    r = i * 32 + u
                    picked[pl.ds(r, 1), :] = wide[pl.ds(lists[0, which, base + r], 1), :]
                return carry

            lax.fori_loop(0, half * block // 32, pick, 0)
            rows = pl.ds(part * half, half)
            packed[slot, rows] = picked[...].astype(jnp.bfloat16).reshape(half, block, snaps)
            number = slot * HALVES + part
            copy = pltpu.make_async_remote_copy(
                src_ref=packed.at[slot, rows],
                dst_ref=cols.at[pl.ds(own + number * half, half)],
                send_sem=ghost_send.at[number],
                recv_sem=ghost_recv.at[number],
                device_id=peer,
                device_id_type=MESH,
            )
            if number == 0:
                pl.semaphore_wait(barrier, len(peers))
            copy.start()
            ghosts.append(copy)

    for load in late:
        load.wait()
    lane = lax.broadcasted_iota(jnp.int32, (1, 2 * block), 1) < block
    for t in range(table.shape[0]):
        both = table[t].astype(jnp.float32)
        pairs[t] = jnp.concatenate([both, both], axis=1)

    def scale_row(i, carry):
        for u in range(WIDE):
            r = i * WIDE + u
            kept = line + r * block < count
            cols[r] = jnp.where(kept, cols[r].astype(jnp.float32), 0.0).astype(jnp.bfloat16)
            for k in range(0, entries - 1, 2):
                one, two = pairs[types[k, r]], pairs[types[k + 1, r]]
                factor = jnp.where(lane, scales[k, r], scales[k + 1, r])
                tile = (jnp.where(lane, one, two) * factor).astype(jnp.bfloat16)
                scaled[r, :, k * block : (k + 2) * block] = tile
            if entries % 2:
                last = pairs[types[entries - 1, r]][:, :block] * scales[entries - 1, r]
                scaled[r, :, (entries - 1) * block :] = last.astype(jnp.bfloat16)
        return carry

    lax.fori_loop(0, own // WIDE, scale_row, 0)
    total[...] = jnp.zeros_like(total)
    weighted[pl.ds(0, STEP)] = jnp.zeros((STEP, block, snaps), jnp.bfloat16)
    for copy in ghosts:
        copy.wait()
    for slot, edge in ((0, 0), (1, bulk_n - 1)):

        @pl.when(b == edge)
        def _():
            first = own + slot * face_blocks
            cols[first : first + face_blocks] = jnp.zeros((face_blocks, block, snaps), jnp.bfloat16)

    def gram_step(i):
        rows = pl.ds(i * STEP, STEP)
        total[...] += lax.dot_general(
            cols[rows].reshape(STEP * block, snaps), weighted[rows].reshape(STEP * block, snaps),
            (((0,), (0,)), ((), ())), preferred_element_type=jnp.float32,
        )

    def mass_step(i, carry):
        gram_step(jnp.maximum(i - 1, 0))
        for u in range(STEP):
            r = i * STEP + u
            stacked = jnp.concatenate([cols[columns[k, r]] for k in range(entries)], axis=0)
            value = jnp.dot(scaled[r], stacked, preferred_element_type=jnp.float32)
            keep = line + r * block < count
            weighted[r] = jnp.where(keep, value, 0.0).astype(jnp.bfloat16)
        return carry

    lax.fori_loop(0, own // STEP, mass_step, 0)
    gram_step(own // STEP - 1)

    def project(phase):
        def one(i, carry):
            here = weighted[pl.ds(i * STEP, STEP)].reshape(STEP * block, snaps)
            rows = pl.ds(pl.multiple_of(i * (STEP * block), STEP * block), STEP * block)
            product = jnp.dot(here, test[...], preferred_element_type=jnp.float32)
            projected[rows, :] = product.astype(jnp.bfloat16)
            return carry

        steps = own // STEP
        first, last = phase * steps // 3, (phase + 1) * steps // 3
        lax.fori_loop(first, last, one, 0)

    for p in range(parts):
        gram[p] = total[p * height : (p + 1) * height, :]
    near[pl.ds(q, 1)] = gram[pl.ds(q, 1)]

    def copy(phase, source, target, peer):
        return pltpu.make_async_remote_copy(
            src_ref=source, dst_ref=target, send_sem=sum_send.at[phase], recv_sem=sum_recv.at[phase],
            device_id=peer, device_id_type=MESH,
        )

    def all_of(phase, buffer):
        some = buffer.at[pl.ds(0, buffer.shape[0] - 1)]
        return copy(phase, some, some, (b, g))

    for d in range(1, parts):
        other, peer = in_plane(d)
        copy(0, gram.at[other], near.at[q], peer).start()
    project(0)
    all_of(0, near).wait_recv()
    far[pl.ds(z, 1)] = jnp.sum(near[...], axis=0, keepdims=True)
    for d in sorted(range(1, depth), key=lambda d: -min(d, depth - d)):
        copy(1, far.at[z], far.at[z], along_z(d)).start()
    project(1)
    all_of(1, far).wait_recv()
    summed[pl.ds(q, 1)] = jnp.sum(far[...], axis=0, keepdims=True)
    for d in range(1, parts):
        copy(2, summed.at[q], summed.at[q], in_plane(d)[1]).start()
    project(2)
    all_of(2, summed).wait_recv()
    all_of(0, near).wait_send()
    all_of(1, far).wait_send()
    all_of(2, summed).wait_send()


def partition_terms(
    snapshots, owned, lists, columns, types, scales, table, test, bulk_n, group_n
):
    rows, snaps = snapshots.shape
    kinds, block, _ = table.shape
    own, entries = columns.shape
    faces = lists.shape[2]
    outer = 4 * faces // block
    parts, depth = NEAR * group_n, bulk_n // NEAR
    height = snaps // parts
    scalar = pl.BlockSpec(memory_space=pltpu.SMEM)
    vmem = pl.BlockSpec(memory_space=pltpu.VMEM)
    return pl.pallas_call(
        functools.partial(partition_kernel, bulk_n, group_n),
        out_shape=(
            pltpu.VMEM((rows, test.shape[1]), jnp.bfloat16),
            pltpu.VMEM((parts, height, snaps), jnp.float32),
        ),
        in_specs=[scalar] + [pl.BlockSpec(memory_space=pltpu.HBM)] * 7,
        out_specs=(vmem, vmem),
        scratch_shapes=[
            pltpu.SMEM(lists.shape, jnp.int32),
            pltpu.SMEM((entries, own), jnp.int32),
            pltpu.SMEM((entries, own), jnp.int32),
            pltpu.SMEM((entries, own), jnp.float32),
            pltpu.VMEM(table.shape, table.dtype),
            pltpu.VMEM(test.shape, test.dtype),
            pltpu.VMEM((own + outer, block, snaps), jnp.bfloat16),
            pltpu.VMEM((rows, snaps), jnp.float32),
            pltpu.VMEM((faces // HALVES, snaps), jnp.float32),
            pltpu.VMEM((4, faces // block, block, snaps), jnp.bfloat16),
            pltpu.VMEM((kinds, block, 2 * block), jnp.float32),
            pltpu.VMEM((own, block, entries * block), jnp.bfloat16),
            pltpu.VMEM((own, block, snaps), jnp.bfloat16),
            pltpu.VMEM((snaps, snaps), jnp.float32),
            pltpu.VMEM((parts, height, snaps), jnp.float32),
            pltpu.VMEM((parts, height, snaps), jnp.float32),
            pltpu.VMEM((depth, height, snaps), jnp.float32),
            pltpu.SemaphoreType.DMA((CHUNKS + 1,)),
            pltpu.SemaphoreType.DMA((5,)),
            pltpu.SemaphoreType.DMA((4 * HALVES,)),
            pltpu.SemaphoreType.DMA((4 * HALVES,)),
            pltpu.SemaphoreType.DMA((3,)),
            pltpu.SemaphoreType.DMA((3,)),
        ],
        compiler_params=pltpu.CompilerParams(
            collective_id=0, has_side_effects=True, vmem_limit_bytes=GRANT - ROOM
        ),
        name="partition_terms",
    )(
        owned,
        *(
            pltpu.with_memory_space_constraint(x, pltpu.HBM)
            for x in (
                lists, columns.T, types.T, scales.T, snapshots.reshape(own, block, snaps), table, test,
            )
        ),
    )


def outputs_kernel(divisor, made, summed, test_hbm, projected, sketch_hbm, test, full, sketch, sems):
    size = made.shape[0] // PIECES
    pieces = [pl.ds(n * size, size) for n in range(PIECES)]
    load = pltpu.make_async_copy(test_hbm, test, sems.at[PIECES])
    stores = [pltpu.make_async_copy(made.at[p], projected.at[p], sems.at[n]) for n, p in enumerate(pieces)]
    for copy in [load] + stores:
        copy.start()
    load.wait()
    parts, height, _ = summed.shape
    for p in range(parts):
        full[p * height : (p + 1) * height, :] = summed[p]
    product = jnp.dot(
        full[...], test[...].astype(jnp.float32),
        precision=lax.Precision.HIGHEST, preferred_element_type=jnp.float32,
    )
    sketch[...] = product / divisor
    last = pltpu.make_async_copy(sketch, sketch_hbm, sems.at[PIECES + 1])
    last.start()
    for copy in stores + [last]:
        copy.wait()


def final_outputs(made, summed, test):
    rows, width = made.shape
    snaps = test.shape[0]
    anywhere = pl.BlockSpec(memory_space=pltpu.HBM)
    vmem = pl.BlockSpec(memory_space=pltpu.VMEM)
    return pl.pallas_call(
        functools.partial(outputs_kernel, rows),
        out_shape=(
            jax.ShapeDtypeStruct((rows, width), jnp.bfloat16),
            jax.ShapeDtypeStruct((snaps, width), jnp.float32),
        ),
        in_specs=[vmem, vmem, anywhere],
        out_specs=(anywhere, anywhere),
        scratch_shapes=[
            pltpu.VMEM(test.shape, jnp.bfloat16),
            pltpu.VMEM((snaps, snaps), jnp.float32),
            pltpu.VMEM((snaps, width), jnp.float32),
            pltpu.SemaphoreType.DMA((PIECES + 2,)),
        ],
        compiler_params=pltpu.CompilerParams(vmem_limit_bytes=GRANT - ROOM),
        name="final_outputs",
    )(made, summed, pltpu.with_memory_space_constraint(test, pltpu.HBM))


def on_device(
    bulk_n, group_n,
    snapshots, owned_rows, iface_lists, block_columns, block_types, block_scales, mass_table, sketch_matrix,
):
    made, summed = partition_terms(
        snapshots, owned_rows, iface_lists, block_columns, block_types, block_scales, mass_table,
        sketch_matrix, bulk_n, group_n,
    )
    return final_outputs(made, summed, sketch_matrix)


def solution(mesh):
    return jax.shard_map(
        functools.partial(on_device, mesh.shape["bulk"], mesh.shape["group"]),
        mesh=mesh,
        in_specs=(
            P(("bulk", "group"), None),
            P(("bulk", "group")),
            P(("bulk", "group"), None, None),
            P(("bulk", "group"), None),
            P(("bulk", "group"), None),
            P(("bulk", "group"), None),
            P(),
            P(),
        ),
        out_specs=(P(("bulk", "group"), None), P()),
        check_vma=False,
    )
```
